256 devices in a mesh: shard: 32 (over z, y), grp: 8 (over x, core).
Axes of the slice: x: 4, y: 4, z: 8, core: 2. Of those that a mesh axis runs over, the one named last changes fastest.
Arguments:
- queries: bfloat16 [8192, 32, 128], P(('shard', 'grp')), may hold values from -0.5 to 0.5
- candidates: int32 [8192, 32], P(('shard', 'grp')), may hold values from 0 to 32767, as said below
- passages: bfloat16 [32768, 128, 128], P(('shard', 'grp')), may hold values from -6 to 6
Outputs:
- scores: float32 [8192, 32], P(('shard', 'grp'))
The draws below stay inside these ranges and needn't reach their ends.
Inputs may be any that keep to these rules, and one draw needn't show every extreme that they name: Passage p is held by the device p // 128 in shard+grp order. One device, the same for all, holds exactly 8 of the 1024 candidates of every device's queries; every other device holds at most 7 of the candidates of any one device's queries.
All inputs are finite; a program needn't handle non-finite values.
Results may differ from the reference program's by a relative error of at most 0.0003.
Values may be sent and summed in bfloat16 or wider, within the bound.
A program may use at most 192 MiB of HBM per device.

```python
import jax
import jax.numpy as jnp
from jax import lax

DIM = 128
QTOK = 32
DTOK = 128
C = 32
Q_DEV = 32
P_DEV = 128
CAP = 8
NQ = 8192
NPASS = 32768
DEVICES = 256


def draw_candidates(key, part):
    key = jax.random.fold_in(key, 7)
    hot_holder = jax.random.randint(jax.random.fold_in(key, 1), (), 0, DEVICES)
    pair_count = Q_DEV * C
    slot_count = DEVICES * CAP
    holders_all = jnp.arange(slot_count, dtype=jnp.int32) // CAP
    within = jnp.arange(slot_count, dtype=jnp.int32) % CAP

    def one_block(block_index):
        block_key = jax.random.fold_in(key, block_index + 2)
        shuffled = jax.random.permutation(jax.random.fold_in(block_key, 0), slot_count).astype(jnp.int32)
        cold_rank = jnp.where(within == CAP - 1, shuffled + slot_count, shuffled)
        ranking = jnp.where(holders_all == hot_holder, within - CAP, cold_rank)
        picked = jnp.argsort(ranking, stable=True)[:pair_count]
        spread = jax.random.permutation(jax.random.fold_in(block_key, 1), pair_count)
        holder = holders_all[picked][spread]
        local_index = jax.random.randint(jax.random.fold_in(block_key, 2), (pair_count,), 0, P_DEV)
        return holder * P_DEV + local_index
    blocks = jax.vmap(one_block)(jnp.arange(DEVICES, dtype=jnp.int32))
    return blocks.reshape(Q_DEV * DEVICES, C).astype(jnp.int32)


def shard_levels(key, shape, pieces, smallest, largest):
    level, own = 1.0, jax.random.fold_in(key, 6)
    for dim, shards_of in pieces:
        draws = jnp.exp(jax.random.uniform(jax.random.fold_in(own, dim), (shards_of,), jnp.float32, smallest / len(pieces), largest / len(pieces)))
        level = level * jnp.repeat(draws, shape[dim] // shards_of).reshape([-1 if axis == dim else 1 for axis in range(len(shape))])
    return level


def bell_draw(stream_key, dims, deviation, reach, cuts=(), kind=jnp.bfloat16):
    gain = shard_levels(stream_key, dims, cuts, -0.22, 0.18) if cuts else 1.0
    result = jax.random.normal(stream_key, dims, jnp.float32) * deviation * gain
    return jnp.minimum(jnp.maximum(result, -reach), reach).astype(kind)


def setup_inputs(seed: int = 0) -> dict:
    arg_keys = jax.random.split(jax.random.key(seed), 4)
    return {
        "queries": bell_draw(arg_keys[0], (NQ, QTOK, DIM), (DIM ** -0.5), 0.5, ((0, 256),)),
        "candidates": draw_candidates(jax.random.fold_in(arg_keys[3], 71), 0),
        "passages": bell_draw(arg_keys[2], (NPASS, DTOK, DIM), 1.0, 6.0, ((0, 256),)),
    }


def reference(queries, candidates, passages):
    def one_block(start):
        query_rows = lax.dynamic_slice_in_dim(queries, start, Q_DEV, 0).astype(jnp.float32)
        cand_ids = lax.dynamic_slice_in_dim(candidates, start, Q_DEV, 0)
        doc_block = passages[cand_ids].astype(jnp.float32)
        similar = jnp.einsum("qid,qcjd->qcij", query_rows, doc_block)
        return jnp.sum(jnp.max(similar, axis=3), axis=2) / QTOK

    starts = jnp.arange(DEVICES, dtype=jnp.int32) * Q_DEV
    return lax.map(one_block, starts).reshape(Q_DEV * DEVICES, C)
```

```python
import functools

import jax
import jax.numpy as jnp
from jax import lax
from jax.experimental import pallas as pl
from jax.experimental.pallas import tpu as pltpu
from jax.sharding import PartitionSpec as P

MESH = pl.DeviceIdType.MESH
NZ, NY, NX = 8, 4, 4
PLANE = NY * NX
CHIPS = NZ * PLANE
QN, QTOK, DIM, DTOK = 32, 32, 128, 128
HALF = QTOK // 2
PAIRS = 1024
P_DEV = 128
SLOTS = 15
LINE = 16


def coords():
    shard, grp = lax.axis_index("shard"), lax.axis_index("grp")
    return shard // NY, shard % NY, grp // 2, grp % 2


def place(z, y, x, c):
    return (z * NY + y, x * 2 + c)


def table_kernel(cand_ref, table_ref, rank_ref):
    cand = cand_ref[...]
    chip = cand // (2 * P_DEV)
    within = cand % (2 * P_DEV)
    onehot = (lax.broadcasted_iota(jnp.int32, (CHIPS, PAIRS), 0) == chip).astype(jnp.bfloat16)
    before = (
        lax.broadcasted_iota(jnp.int32, (128, 128), 0)
        < lax.broadcasted_iota(jnp.int32, (128, 128), 1)
    ).astype(jnp.bfloat16)
    carry = jnp.zeros((CHIPS, 1), jnp.float32)
    ranks = []
    for b in range(PAIRS // 128):
        block = onehot[:, b * 128 : (b + 1) * 128]
        count = jnp.dot(block, before, preferred_element_type=jnp.float32) + carry
        wide = block.astype(jnp.float32)
        ranks.append(jnp.sum(wide * count, axis=0, keepdims=True))
        carry = carry + jnp.sum(wide, axis=1, keepdims=True)
    rank = jnp.concatenate(ranks, axis=1).astype(jnp.int32)
    rank_ref[...] = rank
    lane = (chip % PLANE) * LINE + rank
    spread = (lax.broadcasted_iota(jnp.int32, (PLANE * LINE, PAIRS), 0) == lane).astype(jnp.bfloat16)
    at_z = lax.broadcasted_iota(jnp.int32, (NZ, PAIRS), 0) == chip // PLANE
    query = lax.broadcasted_iota(jnp.int32, (NZ, PAIRS), 1) // QN
    dims = (((1,), (1,)), ((), ()))
    picked = [
        lax.dot_general(
            jnp.where(at_z, value, 0).astype(jnp.float32).astype(jnp.bfloat16),
            spread,
            dims,
            preferred_element_type=jnp.float32,
        ).astype(jnp.int32)
        for value in (query, jnp.broadcast_to(within, (NZ, PAIRS)))
    ]
    table = picked[0] * 256 + picked[1]
    table_ref[:, 0, :] = table[:, :128]
    table_ref[:, 1, :] = table[:, 128:]


def offset_z(t):
    return jnp.where(t % 2 == 0, t // 2, NZ - (t + 1) // 2)


def offset_j(j):
    return jnp.where(j >= 2, 5 - j, j)


def main_kernel(
    q_ref, table_ref, pas_hbm, out_ref,
    ga, gb, sa, sb, ra, rb, pas, stage_a, stage_b, t_line, t_plane, tbl, s_own, s_line,
    ax_send, ax_recv, z_send, z_recv, p_send, p_recv,
    tl_send, tl_recv, tp_send, tp_recv, sl_send, sl_recv, sp_send, sp_recv, pas_sem, loc_sem,
):
    z, y, x, c = coords()
    chip = y * NX + x
    plane = [(dy, dx) for dy in range(NY) for dx in range(NX) if (dy, dx) != (0, 0)]

    def to_z(dz):
        return place((z + dz) % NZ, y, x, c)

    def to_plane(dy, dx):
        return place(z, (y + dy) % NY, (x + dx) % NX, c)

    def copy(src, dst, send, recv, device):
        return pltpu.make_async_remote_copy(
            src_ref=src, dst_ref=dst, send_sem=send, recv_sem=recv, device_id=device, device_id_type=MESH
        )

    sibling = place(z, y, x, 1 - c)
    barrier = pltpu.get_barrier_semaphore()
    everyone = [to_z(dz) for dz in range(1, NZ)] + [to_plane(dy, dx) for dy, dx in plane] + [sibling]
    for device in everyone:
        pl.semaphore_signal(barrier, inc=1, device_id=device, device_id_type=MESH)
    pl.semaphore_wait(barrier, len(everyone))

    def table_line(dz):
        return copy(table_ref.at[(z + dz) % NZ], t_line.at[z], tl_send.at[dz - 1], tl_recv.at[dz - 1], to_z(dz))

    for dz in range(1, NZ):
        table_line(dz).start()
    t_line[z] = table_ref[z]

    def axis_a(o):
        return copy(q_ref.at[:, :HALF], ga.at[z, y], ax_send.at[0, o - 1], ax_recv.at[0, o - 1], to_plane(o, 0))

    def axis_b(o):
        return copy(q_ref.at[:, HALF:], gb.at[z, x], ax_send.at[1, o - 1], ax_recv.at[1, o - 1], to_plane(0, o))

    for o in (1, 3, 2):
        axis_a(o).start()
        axis_b(o).start()
    ga[z, y] = q_ref[:, :HALF]
    gb[z, x] = q_ref[:, HALF:]

    own_pas = pltpu.make_async_copy(pas_hbm, pas.at[pl.ds(c * P_DEV, P_DEV)], loc_sem.at[0])
    own_pas.start()
    their_pas = copy(pas_hbm, pas.at[pl.ds(c * P_DEV, P_DEV)], pas_sem.at[0], pas_sem.at[1], sibling)
    their_pas.start()

    s_own[...] = jnp.zeros_like(s_own)

    def ring(part, t, j, up, late):
        zs = (z + offset_z(t)) % NZ
        buf, sub = (ga, (y + offset_j(j)) % NY) if part == 0 else (gb, (x + offset_j(j)) % NX)
        return copy(
            buf.at[zs, sub], buf.at[zs, sub],
            z_send.at[up, part, t, j], z_recv.at[part, late, j],
            to_z(1 if up else NZ - 1),
        )

    def ring_start(t, j):
        @pl.when(t == 0)
        def _():
            for part in range(2):
                ring(part, t, j, 1, 1).start()
                ring(part, t, j, 0, 2).start()

        for up in range(2):
            @pl.when((t >= 1) & (t <= 4) & (t % 2 == up))
            def _(up=up):
                for part in range(2):
                    ring(part, t, j, up, t + 2).start()

        @pl.when(t == 5)
        def _():
            ring(0, t, j, 1, 7).start()

        @pl.when(t == 6)
        def _():
            ring(1, t, j, 0, 7).start()

    def packed(part, t, j, o):
        zs = (z + offset_z(t)) % NZ
        if part == 0:
            ys = (y + offset_j(j)) % NY
            return copy(
                sa.at[o - 1, t, j], ra.at[zs, ys, x],
                p_send.at[part, t, j, o - 1], p_recv.at[part, t, j, o - 1], to_plane(0, o),
            )
        xs = (x + offset_j(j)) % NX
        return copy(
            sb.at[o - 1, t, j], rb.at[zs, y, xs],
            p_send.at[part, t, j, o - 1], p_recv.at[part, t, j, o - 1], to_plane(o, 0),
        )

    def arrive(t, j):
        @pl.when((t == 0) & (j > 0))
        def _():
            o = offset_j(j)
            for part, buf, sub in ((0, ga, (y + o) % NY), (1, gb, (x + o) % NX)):
                here = buf.at[z, sub]
                copy(here, here, ax_send.at[part, 3 - o], ax_recv.at[part, 3 - o], sibling).wait_recv()

        @pl.when(t > 0)
        def _():
            zs = (z + offset_z(t)) % NZ
            for part, buf, sub in ((0, ga, (y + offset_j(j)) % NY), (1, gb, (x + offset_j(j)) % NX)):
                here = buf.at[zs, sub]
                copy(here, here, z_send.at[0, part, t, j], z_recv.at[part, t, j], sibling).wait_recv()

    def process(t, j):
        zs = (z + offset_z(t)) % NZ
        ys = (y + offset_j(j)) % NY
        xs = (x + offset_j(j)) % NX
        arrive(t, j)
        ring_start(t, j)
        stage_a[...] = ga[zs, ys]
        stage_b[...] = gb[zs, xs]
        for o in (2, 1, 3, 0):
            for part in range(2):
                if part == 0:
                    src, dst, stage = ys * NX + x, y * NX + (x + o) % NX, stage_a
                else:
                    src, dst, stage = y * NX + xs, ((y + o) % NY) * NX + x, stage_b
                for k in range(SLOTS):
                    row = tbl[src, zs, dst // 8, (dst % 8) * LINE + k] // 256
                    value = stage[row]
                    if o > 0:
                        (sa if part == 0 else sb)[o - 1, t, j, k] = value
                    elif part == 0:
                        ra[zs, ys, x, k] = value
                    else:
                        rb[zs, y, xs, k] = value
                if o > 0:
                    packed(part, t, j, o).start()

    lanes = lax.broadcasted_iota(jnp.int32, (8, 128), 1)

    def wait_packed(t):
        @pl.loop(0, 4)
        def _(j):
            for o in range(1, 4):
                for part in range(2):
                    packed_here(part, t, j, o).wait_recv()

    def packed_here(part, t, j, o):
        zs = (z + offset_z(t)) % NZ
        if part == 0:
            here = ra.at[zs, (y + offset_j(j)) % NY, (x + 4 - o) % NX]
        else:
            here = rb.at[zs, (y + 4 - o) % NY, (x + offset_j(j)) % NX]
        return copy(here, here, p_send.at[part, t, j, o - 1], p_recv.at[part, t, j, o - 1], sibling)

    def compute(m):
        t, ys = m // 4, m % 4
        zs = (z + offset_z(t)) % NZ

        @pl.when(ys == 0)
        def _():
            wait_packed(t)

        def source(xs, acc):
            for k in range(SLOTS):
                query = jnp.concatenate([ra[zs, ys, xs, k], rb[zs, ys, xs, k]], axis=0)
                passage = pas[tbl[ys * NX + xs, zs, chip // 8, (chip % 8) * LINE + k] % 256]
                similar = lax.dot_general(
                    query, passage, (((1,), (1,)), ((), ())), preferred_element_type=jnp.float32
                )
                best = jnp.max(similar, axis=1, keepdims=True)
                part = best[0:8] + best[8:16] + best[16:24] + best[24:32]
                acc = jnp.where(lanes == (ys % 2) * 64 + xs * LINE + k, part, acc)
            return acc

        acc = lax.fori_loop(0, NX, source, jnp.zeros((8, 128), jnp.float32))
        row = pl.ds(ys // 2, 1)
        s_own[zs, row] = s_own[zs, row] + jnp.sum(acc, axis=0, keepdims=True) * (1.0 / QTOK)

    for dz in range(1, NZ):
        here = t_line.at[(z + NZ - dz) % NZ]
        copy(here, here, tl_send.at[dz - 1], tl_recv.at[dz - 1], sibling).wait_recv()
    for i, (dy, dx) in enumerate(plane):
        copy(t_line, t_plane.at[chip], tp_send.at[i], tp_recv.at[i], to_plane(dy, dx)).start()
    t_plane[chip] = t_line[...]
    for i, (dy, dx) in enumerate(plane):
        here = t_plane.at[((y + NY - dy) % NY) * NX + (x + NX - dx) % NX]
        copy(here, here, tp_send.at[i], tp_recv.at[i], sibling).wait_recv()
    to_scalar = pltpu.make_async_copy(t_plane, tbl, loc_sem.at[1])
    to_scalar.start()
    to_scalar.wait()

    def unit(u):
        v = jnp.clip(u - 4, 0, 23)
        middle = (u >= 4) & (u < 28)
        t = jnp.where(middle, 2 * (v // 8) + 1 + v % 2, jnp.where(u < 4, 0, 7))
        j = jnp.where(middle, (v % 8) // 2, u % 4)
        process(t, j)

    @pl.loop(0, 8)
    def _(u):
        unit(u)

    own_pas.wait()
    their_pas.wait()

    @pl.loop(8, 28)
    def _(u):
        unit(u)
        compute(u - 8)

    @pl.loop(28, 32)
    def _(u):
        unit(u)

        @pl.loop(0, 2)
        def _(i):
            compute(20 + 2 * (u - 28) + i)

    @pl.loop(28, 32)
    def _(m):
        compute(m)

    for dz in range(1, NZ):
        copy(s_own.at[(z + dz) % NZ], s_line.at[z], sl_send.at[dz - 1], sl_recv.at[dz - 1], to_z(dz)).start()
    s_line[z] = s_own[z]
    for dz in range(1, NZ):
        here = s_line.at[(z + NZ - dz) % NZ]
        copy(here, here, sl_send.at[dz - 1], sl_recv.at[dz - 1], sibling).wait_recv()
    for i, (dy, dx) in enumerate(plane):
        copy(s_line, out_ref.at[chip], sp_send.at[i], sp_recv.at[i], to_plane(dy, dx)).start()
    out_ref[chip] = s_line[...]
    for i, (dy, dx) in enumerate(plane):
        here = out_ref.at[((y + NY - dy) % NY) * NX + (x + NX - dx) % NX]
        copy(here, here, sp_send.at[i], sp_recv.at[i], sibling).wait_recv()

    for dz in range(1, NZ):
        table_line(dz).wait_send()
        copy(s_own.at[(z + dz) % NZ], s_line.at[z], sl_send.at[dz - 1], sl_recv.at[dz - 1], to_z(dz)).wait_send()
    for o in (1, 2, 3):
        axis_a(o).wait_send()
        axis_b(o).wait_send()
    for i, (dy, dx) in enumerate(plane):
        copy(t_line, t_plane.at[chip], tp_send.at[i], tp_recv.at[i], to_plane(dy, dx)).wait_send()
        copy(s_line, out_ref.at[chip], sp_send.at[i], sp_recv.at[i], to_plane(dy, dx)).wait_send()

    @pl.loop(0, 4)
    def _(j):
        for part in range(2):
            ring(part, 0, j, 1, 1).wait_send()
            ring(part, 0, j, 0, 2).wait_send()
            for t in range(1, 5):
                ring(part, t, j, t % 2, t + 2).wait_send()
        ring(0, 5, j, 1, 7).wait_send()
        ring(1, 6, j, 0, 7).wait_send()

    @pl.loop(0, 32)
    def _(n):
        for o in range(1, 4):
            for part in range(2):
                packed(part, n // 4, n % 4, o).wait_send()


def scatter_kernel(d_ref, cand_ref, rank_ref, out_ref):
    _, y, x, _ = coords()
    mine = y * NX + x
    chip = cand_ref[...] // (2 * P_DEV)
    low = d_ref[:, :, 0, :].reshape(CHIPS, 128)
    high = d_ref[:, :, 1, :].reshape(CHIPS, 128)
    rows = jnp.where(mine // 8 == 0, low, high)
    rows = pltpu.roll(rows, (128 - (mine % 8) * LINE) % 128, 1)
    by_slot = rows.T[:LINE]
    holder = (chip % PLANE) * NZ + chip // PLANE
    onehot = (lax.broadcasted_iota(jnp.int32, (CHIPS, PAIRS), 0) == holder).astype(jnp.bfloat16)
    total = jnp.zeros((LINE, PAIRS), jnp.float32)
    left = by_slot
    for _ in range(3):
        piece = left.astype(jnp.bfloat16)
        left = left - piece.astype(jnp.float32)
        total = total + jnp.dot(piece, onehot, preferred_element_type=jnp.float32)
    pick = lax.broadcasted_iota(jnp.int32, (LINE, PAIRS), 0) == rank_ref[...]
    out_ref[...] = jnp.sum(jnp.where(pick, total, 0.0), axis=0, keepdims=True)


def local(queries, candidates, passages):
    vmem = pl.BlockSpec(memory_space=pltpu.VMEM)
    cand = candidates.reshape(1, PAIRS)
    table, rank = pl.pallas_call(
        table_kernel,
        out_shape=(
            jax.ShapeDtypeStruct((NZ, 2, 128), jnp.int32),
            jax.ShapeDtypeStruct((1, PAIRS), jnp.int32),
        ),
        in_specs=[vmem],
        out_specs=(vmem, vmem),
    )(cand)
    bf16, f32, i32 = jnp.bfloat16, jnp.float32, jnp.int32
    dma = pltpu.SemaphoreType.DMA
    returned = pl.pallas_call(
        main_kernel,
        out_shape=jax.ShapeDtypeStruct((PLANE, NZ, 2, 128), f32),
        in_specs=[vmem, vmem, pl.BlockSpec(memory_space=pl.ANY)],
        out_specs=vmem,
        scratch_shapes=[
            pltpu.VMEM((NZ, NY, QN, HALF, DIM), bf16),
            pltpu.VMEM((NZ, NX, QN, HALF, DIM), bf16),
            pltpu.VMEM((3, NZ, 4, SLOTS, HALF, DIM), bf16),
            pltpu.VMEM((3, NZ, 4, SLOTS, HALF, DIM), bf16),
            pltpu.VMEM((NZ, NY, NX, SLOTS, HALF, DIM), bf16),
            pltpu.VMEM((NZ, NY, NX, SLOTS, HALF, DIM), bf16),
            pltpu.VMEM((2 * P_DEV, DTOK, DIM), bf16),
            pltpu.VMEM((QN, HALF, DIM), bf16),
            pltpu.VMEM((QN, HALF, DIM), bf16),
            pltpu.VMEM((NZ, 2, 128), i32),
            pltpu.VMEM((PLANE, NZ, 2, 128), i32),
            pltpu.SMEM((PLANE, NZ, 2, 128), i32),
            pltpu.VMEM((NZ, 2, 128), f32),
            pltpu.VMEM((NZ, 2, 128), f32),
            dma((2, 3)), dma((2, 3)),
            dma((2, 2, 8, 4)), dma((2, 8, 4)),
            dma((2, 8, 4, 3)), dma((2, 8, 4, 3)),
            dma((NZ - 1,)), dma((NZ - 1,)),
            dma((PLANE - 1,)), dma((PLANE - 1,)),
            dma((NZ - 1,)), dma((NZ - 1,)),
            dma((PLANE - 1,)), dma((PLANE - 1,)),
            dma((2,)), dma((2,)),
        ],
        compiler_params=pltpu.CompilerParams(
            collective_id=0, has_side_effects=True, vmem_limit_bytes=60 * 2**20
        ),
    )(queries, table, passages)
    scores = pl.pallas_call(
        scatter_kernel,
        out_shape=jax.ShapeDtypeStruct((1, PAIRS), f32),
        in_specs=[vmem, vmem, vmem],
        out_specs=vmem,
    )(returned, cand, rank)
    return scores.reshape(QN, PAIRS // QN)


def solution(mesh):
    in_specs = (
        P(("shard", "grp"), None, None),
        P(("shard", "grp"), None),
        P(("shard", "grp"), None, None),
    )
    out_specs = P(("shard", "grp"), None)
    return jax.shard_map(local, mesh=mesh, in_specs=in_specs, out_specs=out_specs, check_vma=False)
```

```python
import jax
import jax.numpy as jnp
from jax import lax
from jax.experimental import pallas as pl
from jax.experimental.pallas import tpu as pltpu
from jax.sharding import PartitionSpec as P

MESH = pl.DeviceIdType.MESH
NZ, NY, NX = 8, 4, 4
PLANE = NY * NX
CHIPS = NZ * PLANE
QN, QTOK, DIM, DTOK = 32, 32, 128, 128
HALF = QTOK // 2
PAIRS = 1024
P_DEV = 128
SLOTS = 15
LINE = 16


def coords():
    shard, grp = lax.axis_index("shard"), lax.axis_index("grp")
    return shard // NY, shard % NY, grp // 2, grp % 2


def place(z, y, x, c):
    return (z * NY + y, x * 2 + c)


def pair_rows(cand_ref):
    wide = jnp.concatenate([cand_ref[pl.ds(r, 8, stride=4), :] for r in range(4)], axis=1)
    return [wide[b : b + 1] for b in range(PAIRS // 128)]


def holders(rows):
    chips = lax.broadcasted_iota(jnp.int32, (CHIPS, 128), 0)
    return [(chips == row // (2 * P_DEV)).astype(jnp.float32) for row in rows]


def slot_tables(cand_ref, table_ref, rank_ref):
    rows = pair_rows(cand_ref)
    before = (
        lax.broadcasted_iota(jnp.int32, (128, 128), 0)
        < lax.broadcasted_iota(jnp.int32, (128, 128), 1)
    ).astype(jnp.bfloat16)
    carry = jnp.zeros((CHIPS, 1), jnp.float32)
    totals = [jnp.zeros((NZ, PLANE * LINE), jnp.float32) for _ in range(2)]
    for b, (row, onehot) in enumerate(zip(rows, holders(rows))):
        count = jnp.dot(onehot.astype(jnp.bfloat16), before, preferred_element_type=jnp.float32) + carry
        rank = jnp.sum(onehot * count, axis=0, keepdims=True).astype(jnp.int32)
        carry = carry + jnp.sum(onehot, axis=1, keepdims=True)
        rank_ref[b : b + 1] = rank
        chip, within = row // (2 * P_DEV), row % (2 * P_DEV)
        lane = (chip % PLANE) * LINE + rank
        spread = (lax.broadcasted_iota(jnp.int32, (PLANE * LINE, 128), 0) == lane).astype(jnp.float32)
        at_z = lax.broadcasted_iota(jnp.int32, (NZ, 128), 0) == chip // PLANE
        query = (lax.broadcasted_iota(jnp.int32, (NZ, 128), 1) + b * 128) // QN
        for n, value in enumerate((query, jnp.broadcast_to(within, (NZ, 128)))):
            totals[n] = totals[n] + lax.dot_general(
                jnp.where(at_z, value, 0).astype(jnp.float32).astype(jnp.bfloat16),
                spread.astype(jnp.bfloat16),
                (((1,), (1,)), ((), ())),
                preferred_element_type=jnp.float32,
            )
    table = totals[0].astype(jnp.int32) * 256 + totals[1].astype(jnp.int32)
    table_ref[:, 0, :] = table[:, :128]
    table_ref[:, 1, :] = table[:, 128:]


def scores_to_pairs(cand_ref, rank_ref, landed_ref, out_ref):
    by_slot = landed_ref[...].reshape(CHIPS, 128).T[:LINE]
    pieces = []
    for _ in range(3):
        pieces.append(by_slot.astype(jnp.bfloat16))
        by_slot = by_slot - pieces[-1].astype(jnp.float32)
    rows = pair_rows(cand_ref)
    done = []
    for b, onehot in enumerate(holders(rows)):
        onehot = onehot.astype(jnp.bfloat16)
        total = sum(jnp.dot(p, onehot, preferred_element_type=jnp.float32) for p in pieces)
        pick = lax.broadcasted_iota(jnp.int32, (LINE, 128), 0) == rank_ref[b : b + 1]
        done.append(jnp.sum(jnp.where(pick, total, 0.0), axis=0, keepdims=True))
    wide = jnp.concatenate(done, axis=0)
    for r in range(4):
        out_ref[pl.ds(r, 8, stride=4), :] = wide[:, r * QN : (r + 1) * QN]


def offset_z(t):
    return jnp.where(t % 2 == 0, t // 2, NZ - (t + 1) // 2)


def offset_j(j):
    return jnp.where(j >= 2, 5 - j, j)


def main_kernel(
    q_ref, cand_ref, pas_hbm, out_ref,
    ga, gb, sa, sb, ra, rb, pas, stage_a, stage_b,
    t_own, t_near, t_line, t_plane, tbl_near, tbl, rank_ref, scored, landed,
    ax_send, ax_recv, z_send, z_recv, p_send, p_recv,
    tn_send, tn_recv, tl_send, tl_recv, tp_send, tp_recv, home_sem, pas_sem, loc_sem,
):
    z, y, x, c = coords()
    chip = y * NX + x
    plane = [(dy, dx) for dy in range(NY) for dx in range(NX) if (dy, dx) != (0, 0)]

    def to_z(dz):
        return place((z + dz) % NZ, y, x, c)

    def to_plane(dy, dx):
        return place(z, (y + dy) % NY, (x + dx) % NX, c)

    def copy(src, dst, send, recv, device):
        return pltpu.make_async_remote_copy(
            src_ref=src, dst_ref=dst, send_sem=send, recv_sem=recv, device_id=device, device_id_type=MESH
        )

    sibling = place(z, y, x, 1 - c)
    barrier = pltpu.get_barrier_semaphore()
    everyone = [to_z(dz) for dz in range(1, NZ)] + [to_plane(dy, dx) for dy, dx in plane] + [sibling]
    for device in everyone:
        pl.semaphore_signal(barrier, inc=1, device_id=device, device_id_type=MESH)
    own_pas = pltpu.make_async_copy(pas_hbm, pas.at[pl.ds(c * P_DEV, P_DEV)], loc_sem.at[0])
    own_pas.start()
    ga[z, y] = q_ref[:, :HALF]
    gb[z, x] = q_ref[:, HALF:]
    slot_tables(cand_ref, t_own, rank_ref)
    t_near[chip] = t_own[z]
    t_line[z] = t_own[z]
    pl.semaphore_wait(barrier, len(everyone))

    def table_near(i):
        return copy(t_own.at[z], t_near.at[chip], tn_send.at[i], tn_recv.at[i], to_plane(*plane[i]))

    def table_line(dz):
        return copy(t_own.at[(z + dz) % NZ], t_line.at[z], tl_send.at[dz - 1], tl_recv.at[dz - 1], to_z(dz))

    def table_plane(i):
        return copy(t_line, t_plane.at[chip], tp_send.at[i], tp_recv.at[i], to_plane(*plane[i]))

    for i in range(PLANE - 1):
        table_near(i).start()
    for dz in range(1, NZ):
        table_line(dz).start()

    def axis_a(o):
        return copy(q_ref.at[:, :HALF], ga.at[z, y], ax_send.at[0, o - 1], ax_recv.at[0, o - 1], to_plane(o, 0))

    def axis_b(o):
        return copy(q_ref.at[:, HALF:], gb.at[z, x], ax_send.at[1, o - 1], ax_recv.at[1, o - 1], to_plane(0, o))

    for o in (1, 3, 2):
        axis_a(o).start()
        axis_b(o).start()

    their_pas = copy(pas_hbm, pas.at[pl.ds(c * P_DEV, P_DEV)], pas_sem.at[0], pas_sem.at[1], sibling)
    their_pas.start()

    def ring(part, t, j, up, late):
        zs = (z + offset_z(t)) % NZ
        buf, sub = (ga, (y + offset_j(j)) % NY) if part == 0 else (gb, (x + offset_j(j)) % NX)
        return copy(
            buf.at[zs, sub], buf.at[zs, sub],
            z_send.at[up, part, t, j], z_recv.at[part, late, j],
            to_z(1 if up else NZ - 1),
        )

    def ring_start(t, j):
        @pl.when(t == 0)
        def _():
            for part in range(2):
                ring(part, t, j, 1, 1).start()
                ring(part, t, j, 0, 2).start()

        for up in range(2):
            @pl.when((t >= 1) & (t <= 4) & (t % 2 == up))
            def _(up=up):
                for part in range(2):
                    ring(part, t, j, up, t + 2).start()

        @pl.when(t == 5)
        def _():
            ring(0, t, j, 1, 7).start()

        @pl.when(t == 6)
        def _():
            ring(1, t, j, 0, 7).start()

    def packed(part, t, j, o):
        zs = (z + offset_z(t)) % NZ
        if part == 0:
            ys = (y + offset_j(j)) % NY
            return copy(
                sa.at[o - 1, t, j], ra.at[zs, ys, x],
                p_send.at[part, t, j, o - 1], p_recv.at[part, t, j, o - 1], to_plane(0, o),
            )
        xs = (x + offset_j(j)) % NX
        return copy(
            sb.at[o - 1, t, j], rb.at[zs, y, xs],
            p_send.at[part, t, j, o - 1], p_recv.at[part, t, j, o - 1], to_plane(o, 0),
        )

    def arrive(t, j):
        @pl.when((t == 0) & (j > 0))
        def _():
            o = offset_j(j)
            for part, buf, sub in ((0, ga, (y + o) % NY), (1, gb, (x + o) % NX)):
                here = buf.at[z, sub]
                copy(here, here, ax_send.at[part, 3 - o], ax_recv.at[part, 3 - o], sibling).wait_recv()

        @pl.when(t > 0)
        def _():
            zs = (z + offset_z(t)) % NZ
            for part, buf, sub in ((0, ga, (y + offset_j(j)) % NY), (1, gb, (x + offset_j(j)) % NX)):
                here = buf.at[zs, sub]
                copy(here, here, z_send.at[0, part, t, j], z_recv.at[part, t, j], sibling).wait_recv()

    def process(t, j, near):
        zs = (z + offset_z(t)) % NZ
        ys = (y + offset_j(j)) % NY
        xs = (x + offset_j(j)) % NX
        arrive(t, j)
        ring_start(t, j)
        stage_a[...] = ga[zs, ys]
        stage_b[...] = gb[zs, xs]
        for o in (2, 1, 3, 0):
            for part in range(2):
                if part == 0:
                    src, dst, stage = ys * NX + x, y * NX + (x + o) % NX, stage_a
                else:
                    src, dst, stage = y * NX + xs, ((y + o) % NY) * NX + x, stage_b
                for k in range(SLOTS):
                    lane = (dst % 8) * LINE + k
                    word = tbl_near[src, dst // 8, lane] if near else tbl[src, zs, dst // 8, lane]
                    value = stage[(word >> 8) & (QN - 1)]
                    if o > 0:
                        (sa if part == 0 else sb)[o - 1, t, j, k] = value
                    elif part == 0:
                        ra[zs, ys, x, k] = value
                    else:
                        rb[zs, y, xs, k] = value
                if o > 0:
                    packed(part, t, j, o).start()

    lanes = lax.broadcasted_iota(jnp.int32, (1, 128), 1)

    def home(zs, ys, xs):
        to = (zs * NY + ys) * NX + xs
        return copy(scored.at[to], landed.at[z * PLANE + chip], home_sem.at[0], home_sem.at[1], place(zs, ys, xs, c))

    def compute(m):
        t = m // 4
        zs = (z + offset_z(t)) % NZ
        where = []
        for i in range(4):
            n = 4 * (m % 4) + i
            shell = jnp.where(n >= 9, 3, jnp.where(n >= 4, 2, jnp.where(n >= 1, 1, 0)))
            step = n - shell * shell
            a, b = jnp.minimum(step, shell), jnp.minimum(2 * shell - step, shell)
            ys, xs = (y + offset_j(a)) % NY, (x + offset_j(b)) % NX
            where.append((ys, xs))

            @pl.when(b != 0)
            def _(t=t, a=a, b=b, ys=ys, xs=xs):
                here, o = ra.at[zs, ys, xs], 3 - offset_j(b)
                copy(here, here, p_send.at[0, t, a, o], p_recv.at[0, t, a, o], sibling).wait_recv()

            @pl.when(a != 0)
            def _(t=t, a=a, b=b, ys=ys, xs=xs):
                here, o = rb.at[zs, ys, xs], 3 - offset_j(a)
                copy(here, here, p_send.at[1, t, b, o], p_recv.at[1, t, b, o], sibling).wait_recv()

        for i, (ys, xs) in enumerate(where):
            acc = jnp.zeros((1, 128), jnp.float32)
            for k in range(SLOTS):
                query = jnp.concatenate([ra[zs, ys, xs, k], rb[zs, ys, xs, k]], axis=0)
                passage = pas[tbl[ys * NX + xs, zs, chip // 8, (chip % 8) * LINE + k] & (2 * P_DEV - 1)]
                similar = lax.dot_general(
                    passage, query, (((1,), (1,)), ((), ())), preferred_element_type=jnp.float32
                )
                best = jnp.max(similar, axis=0, keepdims=True)
                acc = jnp.where(lanes == k, jnp.sum(best, axis=1, keepdims=True) * (1.0 / QTOK), acc)
            scored[(zs * NY + ys) * NX + xs] = acc

        for i, (ys, xs) in enumerate(where):
            @pl.when((m > 0) | (i > 0))
            def _(ys=ys, xs=xs):
                home(zs, ys, xs).start()

    for dz in range(1, NZ):
        here = t_line.at[(z + NZ - dz) % NZ]
        copy(here, here, tl_send.at[dz - 1], tl_recv.at[dz - 1], sibling).wait_recv()
    for i in range(PLANE - 1):
        table_plane(i).start()
    t_plane[chip] = t_line[...]

    def from_plane(i):
        dy, dx = plane[i]
        return ((y + NY - dy) % NY) * NX + (x + NX - dx) % NX

    for i in range(PLANE - 1):
        here = t_near.at[from_plane(i)]
        copy(here, here, tn_send.at[i], tn_recv.at[i], sibling).wait_recv()
    to_scalar = pltpu.make_async_copy(t_near, tbl_near, loc_sem.at[1])
    to_scalar.start()
    to_scalar.wait()

    @pl.loop(0, 4)
    def _(j):
        process(0, j, True)

    for i in range(PLANE - 1):
        here = t_plane.at[from_plane(i)]
        copy(here, here, tp_send.at[i], tp_recv.at[i], sibling).wait_recv()
    to_scalar = pltpu.make_async_copy(t_plane, tbl, loc_sem.at[1])
    to_scalar.start()
    to_scalar.wait()

    def unit(u):
        v = jnp.minimum(u - 4, 23)
        middle = u < 28
        t = jnp.where(middle, 2 * (v // 8) + 1 + v % 2, 7)
        j = jnp.where(middle, (v % 8) // 2, u % 4)
        process(t, j, False)

    @pl.loop(4, 8)
    def _(u):
        unit(u)

    own_pas.wait()
    their_pas.wait()

    @pl.loop(8, 28)
    def _(u):
        unit(u)
        compute(u - 8)

    @pl.loop(28, 32)
    def _(u):
        unit(u)

        @pl.loop(0, 2)
        def _(i):
            compute(20 + 2 * (u - 28) + i)

    @pl.loop(28, 32)
    def _(m):
        compute(m)

    own = z * PLANE + chip
    landed[own] = scored[own]
    others = pl.ds(0, CHIPS - 1)
    copy(scored.at[others], landed.at[others], home_sem.at[0], home_sem.at[1], sibling).wait()
    scores_to_pairs(cand_ref, rank_ref, landed, out_ref)

    for dz in range(1, NZ):
        table_line(dz).wait_send()
    for o in (1, 2, 3):
        axis_a(o).wait_send()
        axis_b(o).wait_send()
    for i in range(PLANE - 1):
        table_near(i).wait_send()
        table_plane(i).wait_send()

    @pl.loop(0, 4)
    def _(j):
        for part in range(2):
            ring(part, 0, j, 1, 1).wait_send()
            ring(part, 0, j, 0, 2).wait_send()
            for t in range(1, 5):
                ring(part, t, j, t % 2, t + 2).wait_send()
        ring(0, 5, j, 1, 7).wait_send()
        ring(1, 6, j, 0, 7).wait_send()

    @pl.loop(0, 32)
    def _(n):
        for o in range(1, 4):
            for part in range(2):
                packed(part, n // 4, n % 4, o).wait_send()


def local(queries, candidates, passages):
    vmem = pl.BlockSpec(memory_space=pltpu.VMEM)
    bf16, f32, i32 = jnp.bfloat16, jnp.float32, jnp.int32
    dma = pltpu.SemaphoreType.DMA
    return pl.pallas_call(
        main_kernel,
        out_shape=jax.ShapeDtypeStruct(candidates.shape, f32),
        in_specs=[vmem, vmem, pl.BlockSpec(memory_space=pl.ANY)],
        out_specs=vmem,
        scratch_shapes=[
            pltpu.VMEM((NZ, NY, QN, HALF, DIM), bf16),
            pltpu.VMEM((NZ, NX, QN, HALF, DIM), bf16),
            pltpu.VMEM((3, NZ, 4, SLOTS, HALF, DIM), bf16),
            pltpu.VMEM((3, NZ, 4, SLOTS, HALF, DIM), bf16),
            pltpu.VMEM((NZ, NY, NX, SLOTS, HALF, DIM), bf16),
            pltpu.VMEM((NZ, NY, NX, SLOTS, HALF, DIM), bf16),
            pltpu.VMEM((2 * P_DEV, DTOK, DIM), bf16),
            pltpu.VMEM((QN, HALF, DIM), bf16),
            pltpu.VMEM((QN, HALF, DIM), bf16),
            pltpu.VMEM((NZ, 2, 128), i32),
            pltpu.VMEM((PLANE, 2, 128), i32),
            pltpu.VMEM((NZ, 2, 128), i32),
            pltpu.VMEM((PLANE, NZ, 2, 128), i32),
            pltpu.SMEM((PLANE, 2, 128), i32),
            pltpu.SMEM((PLANE, NZ, 2, 128), i32),
            pltpu.VMEM((PAIRS // 128, 128), i32),
            pltpu.VMEM((CHIPS, 1, 128), f32),
            pltpu.VMEM((CHIPS, 1, 128), f32),
            dma((2, 3)), dma((2, 3)),
            dma((2, 2, 8, 4)), dma((2, 8, 4)),
            dma((2, 8, 4, 3)), dma((2, 8, 4, 3)),
            dma((PLANE - 1,)), dma((PLANE - 1,)),
            dma((NZ - 1,)), dma((NZ - 1,)),
            dma((PLANE - 1,)), dma((PLANE - 1,)),
            dma((2,)), dma((2,)), dma((2,)),
        ],
        compiler_params=pltpu.CompilerParams(
            collective_id=0, has_side_effects=True, vmem_limit_bytes=60 * 2**20
        ),
    )(queries, candidates, passages)


def solution(mesh):
    in_specs = (
        P(("shard", "grp"), None, None),
        P(("shard", "grp"), None),
        P(("shard", "grp"), None, None),
    )
    out_specs = P(("shard", "grp"), None)
    return jax.shard_map(local, mesh=mesh, in_specs=in_specs, out_specs=out_specs, check_vma=False)
```

```python
import jax
import jax.numpy as jnp
from jax import lax
from jax.experimental import pallas as pl
from jax.experimental.pallas import tpu as pltpu
from jax.sharding import PartitionSpec as P

MESH = pl.DeviceIdType.MESH
NZ, NY, NX = 8, 4, 4
PLANE = NY * NX
CHIPS = NZ * PLANE
QN, QTOK, DIM, DTOK = 32, 32, 128, 128
HALF = QTOK // 2
PAIRS = 1024
P_DEV = 128
SLOTS = 15
LINE = 16

HUBS = ((0, 0), (0, 2), (2, 1), (2, 3))
STEPS = (
    ((0, 1), (1, 0), (3, 0)),
    ((0, 1), (1, 0), (3, 0)),
    ((3, 0), (0, 3), (1, 0)),
    ((3, 0), (0, 3), (1, 0)),
)


def swapped(offset, part):
    return offset if part == 0 else offset[::-1]


def code(offset):
    return offset[0] * NX + offset[1]


HUB = [[code(swapped(h, p)) for h in HUBS] for p in range(2)]
STEP = [[[code(swapped(STEPS[j][n], p)) for j in range(4)] for n in range(3)] for p in range(2)]
REACH = [
    [
        [
            code(swapped(((HUBS[j][0] + STEPS[j][n][0]) % NY, (HUBS[j][1] + STEPS[j][n][1]) % NX), p))
            for j in range(4)
        ]
        for n in range(3)
    ]
    for p in range(2)
]
SERVER = [[0] * 16 for _ in range(2)]
for _p in range(2):
    for _j in range(4):
        SERVER[_p][HUB[_p][_j]] = _j
        for _n in range(3):
            SERVER[_p][REACH[_p][_n][_j]] = _j
LAST = [max(SERVER[0][d], SERVER[1][d]) for d in range(16)]
ORDER = sorted(range(16), key=lambda d: (LAST[d], d))
NEEDS = [min(i for i in range(4) if max(LAST[d] for d in ORDER[4 * i : 4 * i + 4]) >= j) for j in range(4)]


def look(values, n):
    words = []
    for start in (0, 8):
        word = sum(v << (4 * i) for i, v in enumerate(values[start : start + 8]))
        words.append(word - 2**32 if word >= 2**31 else word)
    if len(values) <= 8:
        return (jnp.int32(words[0]) >> (4 * n)) & 15
    return (jnp.where(n < 8, jnp.int32(words[0]), jnp.int32(words[1])) >> (4 * (n % 8))) & 15


def coords():
    shard, grp = lax.axis_index("shard"), lax.axis_index("grp")
    return shard // NY, shard % NY, grp // 2, grp % 2


def place(z, y, x, c):
    return (z * NY + y, x * 2 + c)


def pair_rows(cand_ref):
    wide = jnp.concatenate([cand_ref[pl.ds(r, 8, stride=4), :] for r in range(4)], axis=1)
    return [wide[b : b + 1] for b in range(PAIRS // 128)]


def holders(rows):
    chips = lax.broadcasted_iota(jnp.int32, (CHIPS, 128), 0)
    return [(chips == row // (2 * P_DEV)).astype(jnp.float32) for row in rows]


def slot_tables(cand_ref, table_ref, rank_ref):
    rows = pair_rows(cand_ref)
    before = (
        lax.broadcasted_iota(jnp.int32, (128, 128), 0)
        < lax.broadcasted_iota(jnp.int32, (128, 128), 1)
    ).astype(jnp.bfloat16)
    carry = jnp.zeros((CHIPS, 1), jnp.float32)
    totals = [jnp.zeros((NZ, PLANE * LINE), jnp.float32) for _ in range(2)]
    for b, (row, onehot) in enumerate(zip(rows, holders(rows))):
        count = jnp.dot(onehot.astype(jnp.bfloat16), before, preferred_element_type=jnp.float32) + carry
        rank = jnp.sum(onehot * count, axis=0, keepdims=True).astype(jnp.int32)
        carry = carry + jnp.sum(onehot, axis=1, keepdims=True)
        rank_ref[b : b + 1] = rank
        chip, within = row // (2 * P_DEV), row % (2 * P_DEV)
        lane = (chip % PLANE) * LINE + rank
        spread = (lax.broadcasted_iota(jnp.int32, (PLANE * LINE, 128), 0) == lane).astype(jnp.float32)
        at_z = lax.broadcasted_iota(jnp.int32, (NZ, 128), 0) == chip // PLANE
        query = (lax.broadcasted_iota(jnp.int32, (NZ, 128), 1) + b * 128) // QN
        for n, value in enumerate((query, jnp.broadcast_to(within, (NZ, 128)))):
            totals[n] = totals[n] + lax.dot_general(
                jnp.where(at_z, value, 0).astype(jnp.float32).astype(jnp.bfloat16),
                spread.astype(jnp.bfloat16),
                (((1,), (1,)), ((), ())),
                preferred_element_type=jnp.float32,
            )
    table = totals[0].astype(jnp.int32) * 256 + totals[1].astype(jnp.int32)
    table_ref[:, 0, :] = table[:, :128]
    table_ref[:, 1, :] = table[:, 128:]


def scores_to_pairs(cand_ref, rank_ref, landed_ref, out_ref):
    by_slot = landed_ref[...].reshape(CHIPS, 128).T[:LINE]
    pieces = []
    for _ in range(3):
        pieces.append(by_slot.astype(jnp.bfloat16))
        by_slot = by_slot - pieces[-1].astype(jnp.float32)
    rows = pair_rows(cand_ref)
    done = []
    for b, onehot in enumerate(holders(rows)):
        onehot = onehot.astype(jnp.bfloat16)
        total = sum(jnp.dot(p, onehot, preferred_element_type=jnp.float32) for p in pieces)
        pick = lax.broadcasted_iota(jnp.int32, (LINE, 128), 0) == rank_ref[b : b + 1]
        done.append(jnp.sum(jnp.where(pick, total, 0.0), axis=0, keepdims=True))
    wide = jnp.concatenate(done, axis=0)
    for r in range(4):
        out_ref[pl.ds(r, 8, stride=4), :] = wide[:, r * QN : (r + 1) * QN]


def offset_z(t):
    return jnp.where(t % 2 == 0, t // 2, NZ - (t + 1) // 2)


def main_kernel(
    q_ref, cand_ref, pas_hbm, out_ref,
    ga, gb, sa, sb, ra, rb, pas, stage_a, stage_b,
    t_own, t_near, t_line, t_plane, tbl_near, tbl, rank_ref, scored, landed,
    ax_send, ax_recv, z_send, z_recv, p_send, p_recv,
    tn_send, tn_recv, tl_send, tl_recv, tp_send, tp_recv, home_sem, pas_sem, loc_sem,
):
    z, y, x, c = coords()
    chip = y * NX + x
    plane = [(dy, dx) for dy in range(NY) for dx in range(NX) if (dy, dx) != (0, 0)]

    def to_z(dz):
        return place((z + dz) % NZ, y, x, c)

    def to_plane(dy, dx):
        return place(z, (y + dy) % NY, (x + dx) % NX, c)

    def copy(src, dst, send, recv, device):
        return pltpu.make_async_remote_copy(
            src_ref=src, dst_ref=dst, send_sem=send, recv_sem=recv, device_id=device, device_id_type=MESH
        )

    sibling = place(z, y, x, 1 - c)

    def drain(like, sem):
        pltpu.make_async_copy(like, like, sem).wait()

    barrier = pltpu.get_barrier_semaphore()
    everyone = [to_z(dz) for dz in range(1, NZ)] + [to_plane(dy, dx) for dy, dx in plane] + [sibling]
    for device in everyone:
        pl.semaphore_signal(barrier, inc=1, device_id=device, device_id_type=MESH)
    own_pas = pltpu.make_async_copy(pas_hbm, pas.at[pl.ds(c * P_DEV, P_DEV)], loc_sem.at[0])
    own_pas.start()
    ga[0, 0] = q_ref[:, :HALF]
    gb[0, 0] = q_ref[:, HALF:]
    slot_tables(cand_ref, t_own, rank_ref)
    t_near[chip] = t_own[z]
    t_line[z] = t_own[z]
    pl.semaphore_wait(barrier, len(everyone))

    def table_near(i):
        return copy(t_own.at[z], t_near.at[chip], tn_send.at[0], tn_recv.at[0], to_plane(*plane[i]))

    def table_line(dz):
        return copy(t_own.at[(z + dz) % NZ], t_line.at[z], tl_send.at[0], tl_recv.at[0], to_z(dz))

    def table_plane(i):
        return copy(t_line, t_plane.at[chip], tp_send.at[0], tp_recv.at[0], to_plane(*plane[i]))

    for i in range(PLANE - 1):
        table_near(i).start()
    for dz in range(1, NZ):
        table_line(dz).start()

    def shifted(offset, sign=1):
        return (y + sign * (offset // NX) + NY) % NY, (x + sign * (offset % NX) + NX) % NX

    def at(offset):
        ys, xs = shifted(offset)
        return place(z, ys, xs, c)

    def spread(part, j):
        return copy(
            q_ref.at[:, part * HALF : (part + 1) * HALF], (ga, gb)[part].at[0, j],
            ax_send.at[0], ax_recv.at[j], at(HUB[part][j]),
        )

    def spread_start(j):
        spread(0, j).start()
        spread(1, j).start()

    spread_start(1)

    their_pas = copy(pas_hbm, pas.at[pl.ds(c * P_DEV, P_DEV)], pas_sem.at[0], pas_sem.at[1], sibling)
    their_pas.start()

    def ring(part, t, j, up, late):
        buf = (ga, gb)[part]
        return copy(
            buf.at[t, j], buf.at[late, j],
            z_send.at[part], z_recv.at[late, j],
            to_z(1 if up else NZ - 1),
        )

    def ring_start(t, j):
        @pl.when(t == 0)
        def _():
            for part in range(2):
                ring(part, t, j, 1, 1).start()
                ring(part, t, j, 0, 2).start()

        for up in range(2):
            @pl.when((t >= 1) & (t <= 4) & (t % 2 == up))
            def _(up=up):
                for part in range(2):
                    ring(part, t, j, up, t + 2).start()

        @pl.when(t == 5)
        def _():
            ring(0, t, j, 1, 7).start()

        @pl.when(t == 6)
        def _():
            ring(1, t, j, 0, 7).start()

    def packed(part, t, j, n):
        return copy(
            (sa, sb)[part].at[n, t, j], (ra, rb)[part].at[t, look(REACH[part][n], j)],
            p_send.at[part], p_recv.at[t, j], at(look(STEP[part][n], j)),
        )

    def arrive(t, j):
        @pl.when((t == 0) & (j > 0))
        def _():
            drain(ga.at[0, pl.ds(0, 2)], ax_recv.at[j])

        @pl.when(t > 0)
        def _():
            drain(ga.at[t, pl.ds(0, 2)], z_recv.at[t, j])

    def process(t, j, near):
        zs = (z + offset_z(t)) % NZ
        stage_a[...] = ga[t, j]
        stage_b[...] = gb[t, j]
        for n in range(4):
            for part in range(2):
                hub = look(HUB[part], j)
                ys, xs = shifted(hub, -1)
                src = ys * NX + xs
                if n < 3:
                    ys, xs = shifted(look(STEP[part][n], j))
                    dst, put, where = ys * NX + xs, (sa, sb)[part], (n, t, j)
                else:
                    dst, put, where = chip, (ra, rb)[part], (t, hub)
                stage = (stage_a, stage_b)[part]
                row, lane = dst // 8, (dst % 8) * LINE
                for k in range(SLOTS):
                    word = tbl_near[src, row, lane + k] if near else tbl[src, zs, row, lane + k]
                    put[(*where, k)] = stage[(word >> 8) & (QN - 1)]
                if n < 3:
                    packed(part, t, j, n).start()

    lanes = lax.broadcasted_iota(jnp.int32, (1, 128), 1)

    def home(zs, ys, xs):
        to = (zs * NY + ys) * NX + xs
        return copy(scored.at[to], landed.at[z * PLANE + chip], home_sem.at[0], home_sem.at[1], place(zs, ys, xs, c))

    def compute(m):
        t = m // 4
        zs = (z + offset_z(t)) % NZ
        where = []
        for i in range(4):
            offset = look(ORDER, 4 * (m % 4) + i)
            where.append((offset, *shifted(offset, -1)))

        for j in range(4):
            @pl.when(look(NEEDS, j) == m % 4)
            def _(j=j):
                drain(ra.at[t, pl.ds(0, 6)], p_recv.at[t, j])

        for offset, ys, xs in where:
            acc = jnp.zeros((1, 128), jnp.float32)
            for k in range(SLOTS):
                query = jnp.concatenate([ra[t, offset, k], rb[t, offset, k]], axis=0)
                word = tbl[ys * NX + xs, zs, chip // 8, (chip % 8) * LINE + k]
                passage = pas[word & (2 * P_DEV - 1)]
                similar = lax.dot_general(
                    passage, query, (((1,), (1,)), ((), ())), preferred_element_type=jnp.float32
                )
                best = jnp.max(similar, axis=0, keepdims=True)
                acc = jnp.where(lanes == k, jnp.sum(best, axis=1, keepdims=True) * (1.0 / QTOK), acc)
            scored[(zs * NY + ys) * NX + xs] = acc

        for i, (_, ys, xs) in enumerate(where):
            @pl.when((m > 0) | (i > 0))
            def _(ys=ys, xs=xs):
                home(zs, ys, xs).start()

    ring_start(0, 0)

    drain(t_line.at[pl.ds(0, NZ - 1)], tl_recv.at[0])
    spread_start(2)
    for i in range(PLANE - 1):
        table_plane(i).start()
    t_plane[chip] = t_line[...]

    arrive(0, 1)
    spread_start(3)
    ring_start(0, 1)

    drain(t_near.at[pl.ds(0, PLANE - 1)], tn_recv.at[0])
    to_scalar = pltpu.make_async_copy(t_near, tbl_near, loc_sem.at[1])
    to_scalar.start()
    to_scalar.wait()

    @pl.loop(0, 4)
    def _(j):
        @pl.when(j >= 2)
        def _():
            arrive(0, j)
            ring_start(0, j)

        process(0, j, True)

    drain(t_plane.at[pl.ds(0, PLANE - 1)], tp_recv.at[0])
    to_scalar = pltpu.make_async_copy(t_plane, tbl, loc_sem.at[1])
    to_scalar.start()
    to_scalar.wait()

    def unit(u):
        v = jnp.minimum(u - 4, 23)
        middle = u < 28
        t = jnp.where(middle, 2 * (v // 8) + 1 + v % 2, 7)
        j = jnp.where(middle, (v % 8) // 2, u % 4)
        arrive(t, j)
        ring_start(t, j)
        process(t, j, False)

    @pl.loop(4, 8)
    def _(u):
        unit(u)

    own_pas.wait()
    their_pas.wait()

    @pl.loop(8, 28)
    def _(u):
        unit(u)
        compute(u - 8)

    @pl.loop(28, 32)
    def _(u):
        unit(u)

        @pl.loop(0, 2)
        def _(i):
            compute(20 + 2 * (u - 28) + i)

    @pl.loop(28, 32)
    def _(m):
        compute(m)

    own = z * PLANE + chip
    landed[own] = scored[own]
    others = pl.ds(0, CHIPS - 1)
    copy(scored.at[others], landed.at[others], home_sem.at[0], home_sem.at[1], sibling).wait()
    scores_to_pairs(cand_ref, rank_ref, landed, out_ref)

    drain(t_near.at[pl.ds(0, PLANE - 1)], tn_send.at[0])
    drain(t_line.at[pl.ds(0, NZ - 1)], tl_send.at[0])
    drain(t_plane.at[pl.ds(0, PLANE - 1)], tp_send.at[0])
    drain(ga.at[0, pl.ds(0, 3)], ax_send.at[0])
    drain(gb.at[0, pl.ds(0, 3)], ax_send.at[0])
    drain(ga.at[pl.ds(0, NZ - 1)], z_send.at[0])
    drain(gb.at[pl.ds(0, NZ - 1)], z_send.at[1])
    drain(sa, p_send.at[0])
    drain(sb, p_send.at[1])


def local(queries, candidates, passages):
    vmem = pl.BlockSpec(memory_space=pltpu.VMEM)
    bf16, f32, i32 = jnp.bfloat16, jnp.float32, jnp.int32
    dma = pltpu.SemaphoreType.DMA
    return pl.pallas_call(
        main_kernel,
        out_shape=jax.ShapeDtypeStruct(candidates.shape, f32),
        in_specs=[vmem, vmem, pl.BlockSpec(memory_space=pl.ANY)],
        out_specs=vmem,
        scratch_shapes=[
            pltpu.VMEM((NZ, 4, QN, HALF, DIM), bf16),
            pltpu.VMEM((NZ, 4, QN, HALF, DIM), bf16),
            pltpu.VMEM((3, NZ, 4, SLOTS, HALF, DIM), bf16),
            pltpu.VMEM((3, NZ, 4, SLOTS, HALF, DIM), bf16),
            pltpu.VMEM((NZ, PLANE, SLOTS, HALF, DIM), bf16),
            pltpu.VMEM((NZ, PLANE, SLOTS, HALF, DIM), bf16),
            pltpu.VMEM((2 * P_DEV, DTOK, DIM), bf16),
            pltpu.VMEM((QN, HALF, DIM), bf16),
            pltpu.VMEM((QN, HALF, DIM), bf16),
            pltpu.VMEM((NZ, 2, 128), i32),
            pltpu.VMEM((PLANE, 2, 128), i32),
            pltpu.VMEM((NZ, 2, 128), i32),
            pltpu.VMEM((PLANE, NZ, 2, 128), i32),
            pltpu.SMEM((PLANE, 2, 128), i32),
            pltpu.SMEM((PLANE, NZ, 2, 128), i32),
            pltpu.VMEM((PAIRS // 128, 128), i32),
            pltpu.VMEM((CHIPS, 1, 128), f32),
            pltpu.VMEM((CHIPS, 1, 128), f32),
            dma((1,)), dma((4,)),
            dma((2,)), dma((8, 4)),
            dma((2,)), dma((8, 4)),
            dma((1,)), dma((1,)), dma((1,)), dma((1,)), dma((1,)), dma((1,)),
            dma((2,)), dma((2,)), dma((2,)),
        ],
        compiler_params=pltpu.CompilerParams(
            collective_id=0, has_side_effects=True, vmem_limit_bytes=60 * 2**20
        ),
    )(queries, candidates, passages)


def solution(mesh):
    in_specs = (
        P(("shard", "grp"), None, None),
        P(("shard", "grp"), None),
        P(("shard", "grp"), None, None),
    )
    out_specs = P(("shard", "grp"), None)
    return jax.shard_map(local, mesh=mesh, in_specs=in_specs, out_specs=out_specs, check_vma=False)
```

```python
import jax
import jax.numpy as jnp
from jax import lax
from jax.experimental import pallas as pl
from jax.experimental.pallas import tpu as pltpu
from jax.sharding import PartitionSpec as P

MESH = pl.DeviceIdType.MESH
NZ, NY, NX = 8, 4, 4
PLANE = NY * NX
CHIPS = NZ * PLANE
QN, QTOK, DIM, DTOK = 32, 32, 128, 128
HALF = QTOK // 2
PAIRS = 1024
P_DEV = 128
SLOTS = 15
LINE = 16

HUBS = ((0, 0), (0, 2), (2, 1), (2, 3))
STEPS = (
    ((0, 1), (1, 0), (3, 0)),
    ((0, 1), (1, 0), (3, 0)),
    ((3, 0), (0, 3), (1, 0)),
    ((3, 0), (0, 3), (1, 0)),
)


def swapped(offset, part):
    return offset if part == 0 else offset[::-1]


def code(offset):
    return offset[0] * NX + offset[1]


HUB = [[code(swapped(h, p)) for h in HUBS] for p in range(2)]
STEP = [[[code(swapped(STEPS[j][n], p)) for j in range(4)] for n in range(3)] for p in range(2)]
REACH = [
    [
        [
            code(swapped(((HUBS[j][0] + STEPS[j][n][0]) % NY, (HUBS[j][1] + STEPS[j][n][1]) % NX), p))
            for j in range(4)
        ]
        for n in range(3)
    ]
    for p in range(2)
]
SERVER = [[0] * 16 for _ in range(2)]
for _p in range(2):
    for _j in range(4):
        SERVER[_p][HUB[_p][_j]] = _j
        for _n in range(3):
            SERVER[_p][REACH[_p][_n][_j]] = _j
LAST = [max(SERVER[0][d], SERVER[1][d]) for d in range(16)]
ORDER = sorted(range(16), key=lambda d: (LAST[d], d))
NEEDS = [min(i for i in range(4) if max(LAST[d] for d in ORDER[4 * i : 4 * i + 4]) >= j) for j in range(4)]


def look(values, n):
    words = []
    for start in (0, 8):
        word = sum(v << (4 * i) for i, v in enumerate(values[start : start + 8]))
        words.append(word - 2**32 if word >= 2**31 else word)
    if len(values) <= 8:
        return (jnp.int32(words[0]) >> (4 * n)) & 15
    return (jnp.where(n < 8, jnp.int32(words[0]), jnp.int32(words[1])) >> (4 * (n % 8))) & 15


def coords():
    shard, grp = lax.axis_index("shard"), lax.axis_index("grp")
    return shard // NY, shard % NY, grp // 2, grp % 2


def place(z, y, x, c):
    return (z * NY + y, x * 2 + c)


def pair_rows(cand_ref):
    wide = jnp.concatenate([cand_ref[pl.ds(r, 8, stride=4), :] for r in range(4)], axis=1)
    return [wide[b : b + 1] for b in range(PAIRS // 128)]


def holders(rows):
    chips = lax.broadcasted_iota(jnp.int32, (CHIPS, 128), 0)
    return [(chips == row // (2 * P_DEV)).astype(jnp.float32) for row in rows]


def slot_tables(cand_ref, table_ref, rank_ref):
    rows = pair_rows(cand_ref)
    before = (
        lax.broadcasted_iota(jnp.int32, (128, 128), 0)
        < lax.broadcasted_iota(jnp.int32, (128, 128), 1)
    ).astype(jnp.bfloat16)
    carry = jnp.zeros((CHIPS, 1), jnp.float32)
    totals = [jnp.zeros((NZ, PLANE * LINE), jnp.float32) for _ in range(2)]
    for b, (row, onehot) in enumerate(zip(rows, holders(rows))):
        count = jnp.dot(onehot.astype(jnp.bfloat16), before, preferred_element_type=jnp.float32) + carry
        rank = jnp.sum(onehot * count, axis=0, keepdims=True).astype(jnp.int32)
        carry = carry + jnp.sum(onehot, axis=1, keepdims=True)
        rank_ref[b : b + 1] = rank
        chip, within = row // (2 * P_DEV), row % (2 * P_DEV)
        lane = (chip % PLANE) * LINE + rank
        spread = (lax.broadcasted_iota(jnp.int32, (PLANE * LINE, 128), 0) == lane).astype(jnp.float32)
        at_z = lax.broadcasted_iota(jnp.int32, (NZ, 128), 0) == chip // PLANE
        query = (lax.broadcasted_iota(jnp.int32, (NZ, 128), 1) + b * 128) // QN
        for n, value in enumerate((query, jnp.broadcast_to(within, (NZ, 128)))):
            totals[n] = totals[n] + lax.dot_general(
                jnp.where(at_z, value, 0).astype(jnp.float32).astype(jnp.bfloat16),
                spread.astype(jnp.bfloat16),
                (((1,), (1,)), ((), ())),
                preferred_element_type=jnp.float32,
            )
    table = totals[0].astype(jnp.int32) * 256 + totals[1].astype(jnp.int32)
    table_ref[:, 0, :] = table[:, :128]
    table_ref[:, 1, :] = table[:, 128:]


def scores_to_pairs(cand_ref, rank_ref, landed_ref, out_ref):
    by_slot = landed_ref[...].reshape(CHIPS, 128).T[:LINE]
    pieces = []
    for _ in range(3):
        pieces.append(by_slot.astype(jnp.bfloat16))
        by_slot = by_slot - pieces[-1].astype(jnp.float32)
    rows = pair_rows(cand_ref)
    done = []
    for b, onehot in enumerate(holders(rows)):
        onehot = onehot.astype(jnp.bfloat16)
        total = sum(jnp.dot(p, onehot, preferred_element_type=jnp.float32) for p in pieces)
        pick = lax.broadcasted_iota(jnp.int32, (LINE, 128), 0) == rank_ref[b : b + 1]
        done.append(jnp.sum(jnp.where(pick, total, 0.0), axis=0, keepdims=True))
    wide = jnp.concatenate(done, axis=0)
    for r in range(4):
        out_ref[pl.ds(r, 8, stride=4), :] = wide[:, r * QN : (r + 1) * QN]


def offset_z(t):
    return jnp.where(t % 2 == 0, t // 2, NZ - (t + 1) // 2)


def main_kernel(
    q_ref, cand_ref, pas_hbm, out_ref,
    ga, gb, sa, sb, ra, rb, pas, stage_a, stage_b,
    t_own, t_near, t_line, t_plane, tbl_near, tbl, rank_ref, scored, landed,
    ax_send, ax_recv, z_send, z_recv, p_send, p_recv,
    tn_send, tn_recv, tl_send, tl_recv, tp_send, tp_recv, home_sem, pas_sem, loc_sem,
):
    z, y, x, c = coords()
    chip = y * NX + x
    plane = [(dy, dx) for dy in range(NY) for dx in range(NX) if (dy, dx) != (0, 0)]

    def to_z(dz):
        return place((z + dz) % NZ, y, x, c)

    def to_plane(dy, dx):
        return place(z, (y + dy) % NY, (x + dx) % NX, c)

    def copy(src, dst, send, recv, device):
        return pltpu.make_async_remote_copy(
            src_ref=src, dst_ref=dst, send_sem=send, recv_sem=recv, device_id=device, device_id_type=MESH
        )

    sibling = place(z, y, x, 1 - c)

    def drain(like, sem):
        pltpu.make_async_copy(like, like, sem).wait()

    barrier = pltpu.get_barrier_semaphore()
    everyone = [to_z(dz) for dz in range(1, NZ)] + [to_plane(dy, dx) for dy, dx in plane] + [sibling]
    for device in everyone:
        pl.semaphore_signal(barrier, inc=1, device_id=device, device_id_type=MESH)
    own_pas = pltpu.make_async_copy(pas_hbm, pas.at[pl.ds(c * P_DEV, P_DEV)], loc_sem.at[0])
    own_pas.start()
    ga[0, 0] = q_ref[:, :HALF]
    gb[0, 0] = q_ref[:, HALF:]
    slot_tables(cand_ref, t_own, rank_ref)
    t_near[chip] = t_own[z]
    t_line[z] = t_own[z]
    pl.semaphore_wait(barrier, len(everyone))

    def table_near(i):
        return copy(t_own.at[z], t_near.at[chip], tn_send.at[0], tn_recv.at[0], to_plane(*plane[i]))

    def table_line(dz):
        return copy(t_own.at[(z + dz) % NZ], t_line.at[z], tl_send.at[0], tl_recv.at[0], to_z(dz))

    def table_plane(i):
        return copy(t_line, t_plane.at[chip], tp_send.at[0], tp_recv.at[0], to_plane(*plane[i]))

    for i in range(PLANE - 1):
        table_near(i).start()
    for dz in range(1, NZ):
        table_line(dz).start()

    def shifted(offset, sign=1):
        return (y + sign * (offset // NX) + NY) % NY, (x + sign * (offset % NX) + NX) % NX

    def at(offset):
        ys, xs = shifted(offset)
        return place(z, ys, xs, c)

    def spread(part, j):
        return copy(
            q_ref.at[:, part * HALF : (part + 1) * HALF], (ga, gb)[part].at[0, j],
            ax_send.at[0], ax_recv.at[j], at(HUB[part][j]),
        )

    def spread_start(j):
        spread(0, j).start()
        spread(1, j).start()

    spread_start(1)

    their_pas = copy(pas_hbm, pas.at[pl.ds(c * P_DEV, P_DEV)], pas_sem.at[0], pas_sem.at[1], sibling)

    def ring(part, t, j, up, late):
        buf = (ga, gb)[part]
        return copy(
            buf.at[t, j], buf.at[late, j],
            z_send.at[part], z_recv.at[late, j],
            to_z(1 if up else NZ - 1),
        )

    def ring_start(t, j):
        @pl.when(t == 0)
        def _():
            for part in range(2):
                ring(part, t, j, 1, 1).start()
                ring(part, t, j, 0, 2).start()

        for up in range(2):
            @pl.when((t >= 1) & (t <= 4) & (t % 2 == up))
            def _(up=up):
                for part in range(2):
                    ring(part, t, j, up, t + 2).start()

        @pl.when(t == 5)
        def _():
            ring(0, t, j, 1, 7).start()

        @pl.when(t == 6)
        def _():
            ring(1, t, j, 0, 7).start()

    def packed(part, t, j, n):
        return copy(
            (sa, sb)[part].at[n, t, j], (ra, rb)[part].at[t, look(REACH[part][n], j)],
            p_send.at[part], p_recv.at[t, j], at(look(STEP[part][n], j)),
        )

    def arrive(t, j):
        @pl.when((t == 0) & (j > 0))
        def _():
            drain(ga.at[0, pl.ds(0, 2)], ax_recv.at[j])

        @pl.when(t > 0)
        def _():
            drain(ga.at[t, pl.ds(0, 2)], z_recv.at[t, j])

    def process(t, j, near):
        zs = (z + offset_z(t)) % NZ
        stage_a[...] = ga[t, j]
        stage_b[...] = gb[t, j]
        for n in range(4):
            for part in range(2):
                hub = look(HUB[part], j)
                ys, xs = shifted(hub, -1)
                src = ys * NX + xs
                if n < 3:
                    ys, xs = shifted(look(STEP[part][n], j))
                    dst, put, where = ys * NX + xs, (sa, sb)[part], (n, t, j)
                else:
                    dst, put, where = chip, (ra, rb)[part], (t, hub)
                stage = (stage_a, stage_b)[part]
                row, lane = dst // 8, (dst % 8) * LINE
                for k in range(SLOTS):
                    word = tbl_near[src, row, lane + k] if near else tbl[src, zs, row, lane + k]
                    put[(*where, k)] = stage[(word >> 8) & (QN - 1)]
                if n < 3:
                    packed(part, t, j, n).start()

    lanes = lax.broadcasted_iota(jnp.int32, (1, 128), 1)

    def home(zs, ys, xs):
        to = (zs * NY + ys) * NX + xs
        return copy(scored.at[to], landed.at[z * PLANE + chip], home_sem.at[0], home_sem.at[1], place(zs, ys, xs, c))

    def compute(m):
        t = m // 4
        zs = (z + offset_z(t)) % NZ
        where = []
        for i in range(4):
            offset = look(ORDER, 4 * (m % 4) + i)
            where.append((offset, *shifted(offset, -1)))

        for j in range(4):
            @pl.when(look(NEEDS, j) == m % 4)
            def _(j=j):
                drain(ra.at[t, pl.ds(0, 6)], p_recv.at[t, j])

        for offset, ys, xs in where:
            acc = jnp.zeros((1, 128), jnp.float32)
            for k in range(SLOTS):
                query = jnp.concatenate([ra[t, offset, k], rb[t, offset, k]], axis=0)
                word = tbl[ys * NX + xs, zs, chip // 8, (chip % 8) * LINE + k]
                passage = pas[word & (2 * P_DEV - 1)]
                similar = lax.dot_general(
                    passage, query, (((1,), (1,)), ((), ())), preferred_element_type=jnp.float32
                )
                best = jnp.max(similar, axis=0, keepdims=True)
                acc = jnp.where(lanes == k, jnp.sum(best, axis=1, keepdims=True) * (1.0 / QTOK), acc)
            scored[(zs * NY + ys) * NX + xs] = acc

        for i, (_, ys, xs) in enumerate(where):
            @pl.when((m > 0) | (i > 0))
            def _(ys=ys, xs=xs):
                home(zs, ys, xs).start()

    ring_start(0, 0)

    drain(t_line.at[pl.ds(0, NZ - 1)], tl_recv.at[0])
    spread_start(2)
    for i in range(PLANE - 1):
        table_plane(i).start()
    t_plane[chip] = t_line[...]

    arrive(0, 1)
    spread_start(3)
    ring_start(0, 1)

    their_pas.start()
    drain(t_near.at[pl.ds(0, PLANE - 1)], tn_recv.at[0])
    to_scalar = pltpu.make_async_copy(t_near, tbl_near, loc_sem.at[1])
    to_scalar.start()
    to_scalar.wait()

    @pl.loop(0, 4)
    def _(j):
        @pl.when(j >= 2)
        def _():
            arrive(0, j)
            ring_start(0, j)

        process(0, j, True)

    drain(t_plane.at[pl.ds(0, PLANE - 1)], tp_recv.at[0])
    to_scalar = pltpu.make_async_copy(t_plane, tbl, loc_sem.at[1])
    to_scalar.start()
    to_scalar.wait()

    def unit(u):
        v = jnp.minimum(u - 4, 23)
        middle = u < 28
        t = jnp.where(middle, 2 * (v // 8) + 1 + v % 2, 7)
        j = jnp.where(middle, (v % 8) // 2, u % 4)
        arrive(t, j)
        ring_start(t, j)
        process(t, j, False)

    @pl.loop(4, 8)
    def _(u):
        unit(u)

    own_pas.wait()
    their_pas.wait()

    @pl.loop(8, 28)
    def _(u):
        unit(u)
        compute(u - 8)

    @pl.loop(28, 32)
    def _(u):
        unit(u)

        @pl.loop(0, 2)
        def _(i):
            compute(20 + 2 * (u - 28) + i)

    @pl.loop(28, 32)
    def _(m):
        compute(m)

    own = z * PLANE + chip
    landed[own] = scored[own]
    others = pl.ds(0, CHIPS - 1)
    copy(scored.at[others], landed.at[others], home_sem.at[0], home_sem.at[1], sibling).wait()
    scores_to_pairs(cand_ref, rank_ref, landed, out_ref)

    drain(t_near.at[pl.ds(0, PLANE - 1)], tn_send.at[0])
    drain(t_line.at[pl.ds(0, NZ - 1)], tl_send.at[0])
    drain(t_plane.at[pl.ds(0, PLANE - 1)], tp_send.at[0])
    drain(ga.at[0, pl.ds(0, 3)], ax_send.at[0])
    drain(gb.at[0, pl.ds(0, 3)], ax_send.at[0])
    drain(ga.at[pl.ds(0, NZ - 1)], z_send.at[0])
    drain(gb.at[pl.ds(0, NZ - 1)], z_send.at[1])
    drain(sa, p_send.at[0])
    drain(sb, p_send.at[1])


def local(queries, candidates, passages):
    vmem = pl.BlockSpec(memory_space=pltpu.VMEM)
    bf16, f32, i32 = jnp.bfloat16, jnp.float32, jnp.int32
    dma = pltpu.SemaphoreType.DMA
    return pl.pallas_call(
        main_kernel,
        out_shape=jax.ShapeDtypeStruct(candidates.shape, f32),
        in_specs=[vmem, vmem, pl.BlockSpec(memory_space=pl.ANY)],
        out_specs=vmem,
        scratch_shapes=[
            pltpu.VMEM((NZ, 4, QN, HALF, DIM), bf16),
            pltpu.VMEM((NZ, 4, QN, HALF, DIM), bf16),
            pltpu.VMEM((3, NZ, 4, SLOTS, HALF, DIM), bf16),
            pltpu.VMEM((3, NZ, 4, SLOTS, HALF, DIM), bf16),
            pltpu.VMEM((NZ, PLANE, SLOTS, HALF, DIM), bf16),
            pltpu.VMEM((NZ, PLANE, SLOTS, HALF, DIM), bf16),
            pltpu.VMEM((2 * P_DEV, DTOK, DIM), bf16),
            pltpu.VMEM((QN, HALF, DIM), bf16),
            pltpu.VMEM((QN, HALF, DIM), bf16),
            pltpu.VMEM((NZ, 2, 128), i32),
            pltpu.VMEM((PLANE, 2, 128), i32),
            pltpu.VMEM((NZ, 2, 128), i32),
            pltpu.VMEM((PLANE, NZ, 2, 128), i32),
            pltpu.SMEM((PLANE, 2, 128), i32),
            pltpu.SMEM((PLANE, NZ, 2, 128), i32),
            pltpu.VMEM((PAIRS // 128, 128), i32),
            pltpu.VMEM((CHIPS, 1, 128), f32),
            pltpu.VMEM((CHIPS, 1, 128), f32),
            dma((1,)), dma((4,)),
            dma((2,)), dma((8, 4)),
            dma((2,)), dma((8, 4)),
            dma((1,)), dma((1,)), dma((1,)), dma((1,)), dma((1,)), dma((1,)),
            dma((2,)), dma((2,)), dma((2,)),
        ],
        compiler_params=pltpu.CompilerParams(
            collective_id=0, has_side_effects=True, vmem_limit_bytes=60 * 2**20
        ),
    )(queries, candidates, passages)


def solution(mesh):
    in_specs = (
        P(("shard", "grp"), None, None),
        P(("shard", "grp"), None),
        P(("shard", "grp"), None, None),
    )
    out_specs = P(("shard", "grp"), None)
    return jax.shard_map(local, mesh=mesh, in_specs=in_specs, out_specs=out_specs, check_vma=False)
```
